128 devices in a mesh: dp: 8 (over x, core), group: 16 (over z, y).
Axes of the slice: x: 4, y: 4, z: 4, core: 2. Of those that a mesh axis runs over, the one named last changes fastest.
Arguments:
- queries: float32 [49152, 1024], P(('dp', 'group')), parts along dimension 0, may hold values from -8 to 8
- passages: float32 [49152, 1024], P(('dp', 'group')), parts along dimension 0, may hold values from -8 to 8
- positives: int32 [49152], P(('dp', 'group')), parts along dimension 0, may hold values from 0 to 6143, each once
- weights: float32 [49152], P(('dp', 'group')), parts along dimension 0, may hold values from 1 to 16
Outputs:
- losses: float32 [49152], P(('dp', 'group')), parts along dimension 0
- grad_queries: float32 [49152, 1024], P(('dp', 'group')), parts along dimension 0
- grad_passages: float32 [49152, 1024], P(('dp', 'group')), parts along dimension 0
The draws below stay inside these ranges and needn't reach their ends.
There are 8 independent parts, one for each index of `dp`. The reference program is written for one: setup_inputs(seed, part) draws one part's arguments, and reference() takes and returns one part's arrays. A program takes and returns all parts, laid end to end along the dimension named above; each array names one. Nothing has to cross between parts.
Inputs may be any that keep to these rules, and one draw needn't show every extreme that they name: `positives`: each of the 6144 passages is the positive of exactly one query.
All inputs are finite; a program needn't handle non-finite values.
Results may differ from the reference program's by a relative error of at most 0.011.
Values may be sent and summed in bfloat16 or wider, within the bound.
A program may use at most 128 MiB of HBM per device.

```python
import math
import jax
import jax.numpy as jnp
from jax import lax

D = 1024
PAIRS = 6144


def draw_passages(key, part):
    key = jax.random.fold_in(key, 5)
    return jax.random.truncated_normal(key, -6.0, 6.0, (PAIRS, D), jnp.float32)


def draw_queries(key, part):
    key = jax.random.fold_in(key, 3)
    return jax.random.truncated_normal(key, -6.0, 6.0, (PAIRS, D), jnp.float32)


def block_scale(key, extent, pieces, least, top_value):
    def one(dim, parts):
        steps = jax.random.uniform(jax.random.fold_in(jax.random.fold_in(key, 6), dim), (parts,), jnp.float32, least / len(pieces), top_value / len(pieces))
        return jnp.repeat(jnp.exp(steps), extent[dim] // parts).reshape((-1,) + (1,) * (len(extent) - dim - 1))

    loudness = one(*pieces[0])
    for cut in pieces[1:]:
        loudness = loudness * one(*cut)
    return loudness


def setup_inputs(seed: int = 0, part: int = 0) -> dict:
    streams_of = jax.random.split(jax.random.key(seed), 5)
    part_keys = jax.random.split(jax.random.fold_in(streams_of[4], part), 5)
    queries = draw_queries(jax.random.fold_in(jax.random.fold_in(streams_of[4], part), 71), part)
    passages = draw_passages(jax.random.fold_in(jax.random.fold_in(streams_of[4], part), 71), part)
    positives = jax.random.permutation(part_keys[2], PAIRS).astype(jnp.int32)
    weights = jnp.clip(jnp.exp(math.log(16.0) - 2.7725887 * jax.random.uniform(part_keys[3], (PAIRS,), jnp.float32) ** block_scale(part_keys[3], (PAIRS,), ((0, 16),), -0.2, 0.2)), 1.0, 16.0)
    return {"queries": queries, "passages": passages, "positives": positives, "weights": weights}


def reference(queries, passages, positives, weights):
    inv_temp = 2.0 / math.sqrt(D)
    query_half = queries.astype(jnp.bfloat16)
    passage_half = passages.astype(jnp.bfloat16)
    scores = lax.dot_general(query_half, passage_half, (((1,), (1,)), ((), ())), preferred_element_type=jnp.float32) * inv_temp
    row_max = lax.optimization_barrier(jnp.max(scores, axis=1))
    log_total = row_max + jnp.log(lax.optimization_barrier(jnp.sum(jnp.exp(scores - row_max[:, None]), axis=1)))
    columns = jnp.arange(PAIRS, dtype=jnp.int32)
    is_positive = columns[None, :] == positives[:, None]
    positive_score = lax.optimization_barrier(jnp.sum(jnp.where(is_positive, scores, 0.0), axis=1))
    losses = log_total - positive_score
    row_weight = weights * inv_temp
    coefficient = (row_weight[:, None] * (jnp.exp(scores - log_total[:, None]) - is_positive.astype(jnp.float32))).astype(jnp.bfloat16)
    grad_queries = jnp.dot(coefficient, passage_half, preferred_element_type=jnp.float32)
    grad_passages = lax.dot_general(coefficient, query_half, (((0,), (0,)), ((), ())), preferred_element_type=jnp.float32)
    return (losses, grad_queries, grad_passages)
```

```python
import functools
import math

import jax
import jax.numpy as jnp
from jax import lax
from jax.experimental import pallas as pl
from jax.experimental.pallas import tpu as pltpu
from jax.sharding import PartitionSpec as P

MESH = pl.DeviceIdType.MESH
SIDE = 4
OWN, NEXT, PREV, FAR = range(4)
STEP = (0, 1, 3, 2)
SEEN = tuple(tuple(STEP.index((STEP[s] + STEP[k]) % SIDE) for k in range(SIDE)) for s in range(SIDE))
LOG2E = math.log2(math.e)
BF16, F32 = jnp.bfloat16, jnp.float32


def kernel(
    rows, width, inv_temp,
    q_hbm, p_hbm, pos_ref, w_ref,
    loss_ref, gq_ref, gp_ref,
    stage, gathered, scores, coef, coef_t, meta, pos_all, stats, peak, shift, partial, sent, hop1, hop2,
    load_sem, ag_send, ag_recv, meta_send, meta_recv, st_send, st_recv, rs_send, rs_recv, go_sem,
):
    half, quarter = rows // 2, rows // 4
    total = SIDE * rows
    rate = inv_temp * LOG2E
    dp, me = lax.axis_index("dp"), lax.axis_index("group")
    z, y = me // SIDE, me % SIDE
    first = dp % 2 == 0
    sibling = dp + 1 - 2 * (dp % 2)

    def at(axis, slot):
        if axis == 0:
            return (dp, z * SIDE + (y + STEP[slot]) % SIDE)
        return (dp, (z + STEP[slot]) % SIDE * SIDE + y)

    greet = [at(0, NEXT), at(0, PREV), at(0, FAR), at(1, NEXT), at(1, PREV), (sibling, me)]
    barrier = pltpu.get_barrier_semaphore()
    for device in greet:
        pl.semaphore_signal(barrier, inc=1, device_id=device, device_id_type=MESH)

    loads = [pltpu.make_async_copy((q_hbm, p_hbm)[a], stage.at[a], load_sem.at[a]) for a in range(2)]
    for load in loads:
        load.start()
    meta[OWN] = jnp.zeros(meta.shape[1:], F32)
    meta[OWN, 0:1, :] = pos_ref[...].astype(F32)
    meta[OWN, 1:2, :] = w_ref[...]

    for a in range(2):
        loads[a].wait()

        @pl.loop(0, rows // 64)
        def _(i):
            part = pl.ds(pl.multiple_of(i * 64, 64), 64)
            gathered[a, part, :] = stage[a, part, :].astype(BF16)

    pl.semaphore_wait(barrier, len(greet))

    @pl.when(jnp.logical_not(first))
    def _():
        pl.semaphore_wait(go_sem, 1)

    def block(slot, h=None):
        if h is None:
            return pl.ds(slot * rows, rows)
        return pl.ds(slot * rows + h * half, half)

    def remote(src, dst, send, recv, device):
        return pltpu.make_async_remote_copy(
            src_ref=src, dst_ref=dst, send_sem=send, recv_sem=recv, device_id=device, device_id_type=MESH
        )

    metas = [
        remote(meta.at[OWN], meta.at[STEP.index(-STEP[s] % SIDE)], meta_send.at[s], meta_recv.at[s], at(0, s))
        for s in (NEXT, PREV, FAR)
    ]
    for copy in metas:
        copy.start()

    def ag(a, d, k):
        h = (0, 1, 0)[k] if d == 0 else (1, 0, 1)[k]
        near = (NEXT, PREV)[d]
        src, dst = (OWN, near) if k < 2 else (near, FAR)
        return remote(
            gathered.at[a, block(src, h)], gathered.at[a, block(dst, h)],
            ag_send.at[a, d, k], ag_recv.at[a, d, k], at(a, (PREV, NEXT)[d]),
        )

    pairs = [(a, d) for d in range(2) for a in (1, 0)]
    for k in range(2):
        for a, d in pairs:
            ag(a, d, k).start()

    peak[...] = jnp.full(peak.shape, -jnp.inf, F32)

    def score(j, i0, cols):
        part = pl.ds(pl.multiple_of(j * quarter, quarter), quarter)
        r = lax.dot_general(
            gathered[1, part, :], gathered[0, i0 : i0 + cols, :], (((1,), (1,)), ((), ())),
            preferred_element_type=F32,
        )
        scores[part, i0 : i0 + cols] = r
        top = jnp.max(r.reshape(quarter // 8, 8, cols), axis=0)
        peak[:, i0 : i0 + cols] = jnp.maximum(peak[:, i0 : i0 + cols], top)

    @pl.loop(0, 4)
    def _(j):
        score(j, 0, rows)

    for a, d in pairs:
        ag(a, d, 0).wait_recv()
        ag(a, d, 2).start()
    for a, d in pairs:
        ag(a, d, 0).wait_send()
        ag(a, d, 1).wait_send()

    @pl.when(first)
    def _():
        pl.semaphore_signal(go_sem, inc=1, device_id=(sibling, me), device_id_type=MESH)

    for a, d in pairs:
        ag(a, d, 1).wait_recv()

    @pl.loop(0, 4)
    def _(j):
        score(j, rows, 2 * rows)

    @pl.loop(4, 12)
    def _(j):
        score(j, 0, 3 * rows)

    for copy in metas:
        copy.wait()
    for s in range(SIDE):
        pos_all[:, block(s)] = jnp.broadcast_to(meta[s, 0:1, :], (8, rows)).astype(jnp.int32)

    for a, d in pairs:
        ag(a, d, 2).wait_recv()

    @pl.loop(0, 12)
    def _(j):
        score(j, 3 * rows, rows)

    @pl.loop(12, 16)
    def _(j):
        score(j, 0, total)

    top = jnp.max(peak[...], axis=0, keepdims=True)
    shift[0:1, :] = top
    zero = jnp.zeros((8, total), F32)
    strip = 16
    wide = rows
    peak[...] = zero
    shift[8:16, :] = zero

    def base(slot):
        owner = (z + STEP[slot]) % SIDE * SIDE + y
        return owner * rows

    for s in range(SIDE):

        @pl.loop(0, rows // strip)
        def _(i):
            part = pl.ds(pl.multiple_of(s * rows + i * strip, strip), strip)
            for c in range(0, total, wide):
                cols = pl.ds(c, wide)
                r = scores[part, cols]
                e = jnp.exp2((r - shift[0:1, cols]) * rate)
                hit = lax.broadcasted_iota(jnp.int32, (strip, wide), 0) == pos_all[0:1, cols] - (base(s) + i * strip)
                g = jnp.where(hit, r, 0.0)
                peak[:, cols] += jnp.sum(e.reshape(strip // 8, 8, wide), axis=0)
                shift[8:16, cols] += jnp.sum(g.reshape(strip // 8, 8, wide), axis=0)

    for s in range(SIDE):
        cols = block(s)
        stats[OWN, s] = jnp.zeros(stats.shape[2:], F32)
        stats[OWN, s, 0:1, :] = shift[0:1, cols]
        stats[OWN, s, 1:2, :] = jnp.sum(peak[:, cols], axis=0, keepdims=True)
        stats[OWN, s, 2:3, :] = jnp.sum(shift[8:16, cols], axis=0, keepdims=True)
    posts = [
        remote(stats.at[OWN], stats.at[STEP.index(-STEP[s] % SIDE)], st_send.at[s], st_recv.at[s], at(0, s))
        for s in (NEXT, PREV, FAR)
    ]
    for copy in posts:
        copy.start()
    for copy in posts:
        copy.wait()
    for k in range(SIDE):
        mine = [stats[s, SEEN[s].index(k)] for s in range(SIDE)]
        top = functools.reduce(jnp.maximum, [m[0:1] for m in mine])
        mass = sum(m[1:2] * jnp.exp2((m[0:1] - top) * rate) for m in mine)
        scale = meta[k, 1:2, :] * inv_temp
        shift[0:1, block(k)] = top + (jnp.log2(mass) - jnp.log2(scale)) * (1.0 / rate)
        shift[1:2, block(k)] = scale
        if k == OWN:
            hit = sum(m[2:3] for m in mine)
            loss_ref[...] = (top - hit) * inv_temp + jnp.log(mass)

    def coefficients(s, i0, cols):
        @pl.loop(0, rows // strip)
        def _(i):
            part = pl.ds(pl.multiple_of(s * rows + i * strip, strip), strip)
            for c in range(i0, i0 + cols, wide):
                lanes = pl.ds(c, wide)
                e = jnp.exp2((scores[part, lanes] - shift[0:1, lanes]) * rate)
                hit = lax.broadcasted_iota(jnp.int32, (strip, wide), 0) == pos_all[0:1, lanes] - (base(s) + i * strip)
                coef[part, lanes] = (e - jnp.where(hit, shift[1:2, lanes], 0.0)).astype(BF16)

    def turn(k):
        @pl.loop(0, SIDE)
        def _(s):
            part = pl.ds(pl.multiple_of(s * rows, rows), rows)
            coef_t[k * rows : (k + 1) * rows, part] = coef[part, k * rows : (k + 1) * rows].T

    tile = min(width, 256)

    def product(a, k, put):
        @pl.loop(0, width // tile)
        def _(n):
            cols = pl.ds(pl.multiple_of(n * tile, tile), tile)
            lhs = coef_t if a == 0 else coef
            r = jnp.dot(
                lhs[k * rows : (k + 1) * rows, :], gathered[1 - a, :, cols], preferred_element_type=F32
            )
            put(r, cols)

    def rs(a, d, k):
        h = (d, d, 1 - d, d, d)[k]
        if k < 2:
            rows_of = pl.ds(h * half + k * quarter, quarter)
            src, dst = sent.at[a, 2, rows_of], hop1.at[a, d, pl.ds(k * quarter, quarter)]
        elif k == 2:
            rows_of = pl.ds(h * half, half)
            src, dst = sent.at[a, d, rows_of], hop2.at[a, d, rows_of]
        else:
            rows_of = pl.ds(h * half + (k - 3) * quarter, quarter)
            src, dst = sent.at[a, d, rows_of], hop2.at[a, d, rows_of]
        return remote(src, dst, rs_send.at[a, d, k], rs_recv.at[a, d, k], at(a, (PREV, NEXT)[d]))

    def far(a):
        def put(r, cols):
            sent[a, 2, :, cols] = r.astype(BF16)

        product(a, FAR, put)
        for k in range(2):
            for d in range(2):
                rs(a, d, k).start()

    def near(a, d):
        def put(r, cols):
            keep = r[half:, :] if d == 1 else r[:half, :]
            send = r[:half, :] if d == 1 else r[half:, :]
            partial[a, d, :, cols] = keep
            sent[a, d, (1 - d) * half : (2 - d) * half, cols] = send.astype(BF16)

        product(a, (PREV, NEXT)[d], put)
        rs(a, d, 2).start()

    def own(a):
        out = (gq_ref, gp_ref)[a]

        def put(r, cols):
            out[:, cols] = r

        product(a, OWN, put)

    def pass_on(a, d, k):
        rs(a, d, k).wait_recv()
        rows_of = slice(d * half + k * quarter, d * half + (k + 1) * quarter)
        sent[a, d, rows_of, :] = (
            partial[a, d, k * quarter : (k + 1) * quarter, :]
            + hop1[a, d, k * quarter : (k + 1) * quarter, :].astype(F32)
        ).astype(BF16)
        rs(a, d, k + 3).start()

    coefficients(FAR, 0, total)
    far(1)
    for s in (OWN, NEXT, PREV):
        coefficients(s, 3 * rows, rows)
    turn(FAR)
    far(0)
    for s in (NEXT, PREV, OWN):
        coefficients(s, 0, 3 * rows)
    for d in range(2):
        near(1, d)
    turn(PREV)
    near(0, 0)
    turn(NEXT)
    near(0, 1)
    for k in range(2):
        for a in (1, 0):
            for d in range(2):
                pass_on(a, d, k)
    turn(OWN)
    own(1)
    own(0)

    def add(a, d, k):
        rs(a, d, k).wait_recv()
        out = (gq_ref, gp_ref)[a]
        h = (d, d, 1 - d, d, d)[k]
        start, size = (h * half, half) if k == 2 else (h * half + (k - 3) * quarter, quarter)
        out[start : start + size, :] += hop2[a, d, start : start + size, :].astype(F32)

    for k in (2, 3, 4):
        for a in (1, 0):
            for d in range(2):
                add(a, d, k)

    for a, d in pairs:
        ag(a, d, 2).wait_send()
        for k in range(5):
            rs(a, d, k).wait_send()


def per_device(queries, passages, positives, weights):
    rows, width = queries.shape
    total = SIDE * rows
    inv_temp = 2.0 / math.sqrt(width)
    vmem = pl.BlockSpec(memory_space=pltpu.VMEM)
    hbm = pl.BlockSpec(memory_space=pl.ANY)
    dma = pltpu.SemaphoreType.DMA
    losses, grad_queries, grad_passages = pl.pallas_call(
        functools.partial(kernel, rows, width, inv_temp),
        out_shape=(
            jax.ShapeDtypeStruct((1, rows), F32),
            jax.ShapeDtypeStruct((rows, width), F32),
            jax.ShapeDtypeStruct((rows, width), F32),
        ),
        in_specs=[hbm, hbm, vmem, vmem],
        out_specs=(vmem, vmem, vmem),
        scratch_shapes=[
            pltpu.VMEM((2, rows, width), F32),
            pltpu.VMEM((2, total, width), BF16),
            pltpu.VMEM((total, total), F32),
            pltpu.VMEM((total, total), BF16),
            pltpu.VMEM((total, total), BF16),
            pltpu.VMEM((SIDE, 8, rows), F32),
            pltpu.VMEM((8, total), jnp.int32),
            pltpu.VMEM((SIDE, SIDE, 8, rows), F32),
            pltpu.VMEM((8, total), F32),
            pltpu.VMEM((16, total), F32),
            pltpu.VMEM((2, 2, rows // 2, width), F32),
            pltpu.VMEM((2, 3, rows, width), BF16),
            pltpu.VMEM((2, 2, rows // 2, width), BF16),
            pltpu.VMEM((2, 2, rows, width), BF16),
            dma((2,)),
            dma((2, 2, 3)),
            dma((2, 2, 3)),
            dma((SIDE,)),
            dma((SIDE,)),
            dma((SIDE,)),
            dma((SIDE,)),
            dma((2, 2, 5)),
            dma((2, 2, 5)),
            pltpu.SemaphoreType.REGULAR,
        ],
        compiler_params=pltpu.CompilerParams(
            collective_id=0, has_side_effects=True, vmem_limit_bytes=60 * 2**20
        ),
    )(queries, passages, positives.reshape(1, rows), weights.reshape(1, rows))
    return losses.reshape(rows), grad_queries, grad_passages


def solution(mesh):
    split = P(("dp", "group"))
    whole = P(("dp", "group"), None)
    return jax.shard_map(
        per_device,
        mesh=mesh,
        in_specs=(whole, whole, split, split),
        out_specs=(split, whole, whole),
        check_vma=False,
    )
```

```python
import functools
import math

import jax
import jax.numpy as jnp
from jax import lax
from jax.experimental import pallas as pl
from jax.experimental.pallas import tpu as pltpu
from jax.sharding import PartitionSpec as P

MESH = pl.DeviceIdType.MESH
SIDE = 4
OWN, NEXT, PREV, FAR = range(4)
STEP = (0, 1, 3, 2)
SEEN = tuple(tuple(STEP.index((STEP[s] + STEP[k]) % SIDE) for k in range(SIDE)) for s in range(SIDE))
LOG2E = math.log2(math.e)
BF16, F32 = jnp.bfloat16, jnp.float32


def kernel(
    rows, width, inv_temp,
    q_hbm, p_hbm, pos_ref, w_ref,
    loss_ref, gq_ref, gp_ref,
    stage, gathered, scores, coef, coef_t, meta, pos_all, stats, peak, mass, found, shift, partial, sent, hop1, hop2,
    load_sem, ag_send, ag_recv, meta_send, meta_recv, st_send, st_recv, rs_send, rs_recv, go_sem,
):
    half, quarter = rows // 2, rows // 4
    total = SIDE * rows
    rate = inv_temp * LOG2E
    dp, me = lax.axis_index("dp"), lax.axis_index("group")
    z, y = me // SIDE, me % SIDE
    first = dp % 2 == 0
    sibling = dp + 1 - 2 * (dp % 2)

    def at(axis, slot):
        if axis == 0:
            return (dp, z * SIDE + (y + STEP[slot]) % SIDE)
        return (dp, (z + STEP[slot]) % SIDE * SIDE + y)

    greet = [at(0, NEXT), at(0, PREV), at(0, FAR), at(1, NEXT), at(1, PREV), (sibling, me)]
    barrier = pltpu.get_barrier_semaphore()
    for device in greet:
        pl.semaphore_signal(barrier, inc=1, device_id=device, device_id_type=MESH)

    loads = [pltpu.make_async_copy((q_hbm, p_hbm)[a], stage.at[a], load_sem.at[a]) for a in range(2)]
    for load in loads:
        load.start()
    meta[OWN] = jnp.zeros(meta.shape[1:], F32)
    meta[OWN, 0:1, :] = pos_ref[...].reshape(1, rows).astype(F32)
    meta[OWN, 1:2, :] = w_ref[...].reshape(1, rows)

    for a in range(2):
        loads[a].wait()

        @pl.loop(0, rows // 64)
        def _(i):
            part = pl.ds(pl.multiple_of(i * 64, 64), 64)
            gathered[a, part, :] = stage[a, part, :].astype(BF16)

    pl.semaphore_wait(barrier, len(greet))

    @pl.when(jnp.logical_not(first))
    def _():
        pl.semaphore_wait(go_sem, 1)

    def block(slot, h=None):
        if h is None:
            return pl.ds(slot * rows, rows)
        return pl.ds(slot * rows + h * half, half)

    def remote(src, dst, send, recv, device):
        return pltpu.make_async_remote_copy(
            src_ref=src, dst_ref=dst, send_sem=send, recv_sem=recv, device_id=device, device_id_type=MESH
        )

    metas = [
        remote(meta.at[OWN], meta.at[STEP.index(-STEP[s] % SIDE)], meta_send.at[s], meta_recv.at[s], at(0, s))
        for s in (NEXT, PREV, FAR)
    ]
    for copy in metas:
        copy.start()

    def ag(a, d, k):
        near = (NEXT, PREV)[d]
        if k < 2:
            h = (k, 1 - k)[d]
            src, dst = block(OWN, h), block(near, h)
        else:
            start, size = d * half + (k - 2) * quarter, quarter
            src, dst = pl.ds(near * rows + start, size), pl.ds(FAR * rows + start, size)
        return remote(
            gathered.at[a, src], gathered.at[a, dst],
            ag_send.at[a, d, k], ag_recv.at[a, d, k], at(a, (PREV, NEXT)[d]),
        )

    pairs = [(a, d) for d in range(2) for a in (1, 0)]
    for k in range(2):
        for a, d in pairs:
            ag(a, d, k).start()

    def base(slot):
        owner = (z + STEP[slot]) % SIDE * SIDE + y
        return owner * rows

    def score(j0, i0, deep, wide):
        r = lax.dot_general(
            gathered[1, j0 : j0 + deep, :], gathered[0, i0 : i0 + wide, :], (((1,), (1,)), ((), ())),
            preferred_element_type=F32,
        )
        scores[j0 : j0 + deep, i0 : i0 + wide] = r
        top = jnp.max(r.reshape(deep // 8, 8, wide), axis=0)
        peak[:, i0 : i0 + wide] = jnp.maximum(peak[:, i0 : i0 + wide], top)

    def settle(i0, wide):
        cols = slice(i0, i0 + wide)
        top = jnp.max(peak[:, cols], axis=0, keepdims=True)
        mass[:, cols] = mass[:, cols] * jnp.exp2((shift[0:1, cols] - top) * rate)
        shift[0:1, cols] = top

    strip = 32

    def accumulate(s, i0, cols):
        @pl.loop(0, rows // strip)
        def _(i):
            part = pl.ds(pl.multiple_of(s * rows + i * strip, strip), strip)
            for c in range(i0, i0 + cols, rows):
                lanes = pl.ds(c, rows)
                r = scores[part, lanes]
                e = jnp.exp2((r - shift[0:1, lanes]) * rate)
                hit = lax.broadcasted_iota(jnp.int32, (strip, rows), 0) == pos_all[0:1, lanes] - (base(s) + i * strip)
                g = jnp.where(hit, r, 0.0)
                mass[:, lanes] += jnp.sum(e.reshape(strip // 8, 8, rows), axis=0)
                found[:, lanes] += jnp.sum(g.reshape(strip // 8, 8, rows), axis=0)

    peak[...] = jnp.full(peak.shape, -jnp.inf, F32)
    shift[...] = jnp.full(shift.shape, -jnp.inf, F32)
    mass[...] = jnp.zeros(mass.shape, F32)
    found[...] = jnp.zeros(found.shape, F32)
    score(0, 0, rows, rows)

    for a, d in pairs:
        ag(a, d, 0).wait_recv()
        ag(a, d, 2).start()
        ag(a, d, 3).start()
    for a, d in pairs:
        for k in range(3):
            ag(a, d, k).wait_send()

    @pl.when(first)
    def _():
        pl.semaphore_signal(go_sem, inc=1, device_id=(sibling, me), device_id_type=MESH)

    for copy in metas:
        copy.wait()
    for s in range(SIDE):
        pos_all[:, block(s)] = jnp.broadcast_to(meta[s, 0:1, :], (8, rows)).astype(jnp.int32)
    for a, d in pairs:
        ag(a, d, 1).wait_recv()

    score(rows, 0, 2 * rows, 3 * rows)
    score(0, rows, rows, 2 * rows)
    settle(0, 3 * rows)
    for s in (OWN, NEXT, PREV):
        accumulate(s, 0, 3 * rows)

    for a, d in pairs:
        for k in (2, 3):
            ag(a, d, k).wait_recv()

    score(3 * rows, 0, rows, 2 * rows)
    score(3 * rows, 2 * rows, rows, 2 * rows)
    score(0, 3 * rows, 3 * rows, rows)
    settle(0, total)
    accumulate(FAR, 0, total)
    for s in (OWN, NEXT, PREV):
        accumulate(s, 3 * rows, rows)

    for s in range(SIDE):
        cols = block(s)
        stats[OWN, s] = jnp.zeros(stats.shape[2:], F32)
        stats[OWN, s, 0:1, :] = shift[0:1, cols]
        stats[OWN, s, 1:2, :] = jnp.sum(mass[:, cols], axis=0, keepdims=True)
        stats[OWN, s, 2:3, :] = jnp.sum(found[:, cols], axis=0, keepdims=True)
    posts = [
        remote(stats.at[OWN], stats.at[STEP.index(-STEP[s] % SIDE)], st_send.at[s], st_recv.at[s], at(0, s))
        for s in (NEXT, PREV, FAR)
    ]
    for copy in posts:
        copy.start()
    for copy in posts:
        copy.wait()
    for k in range(SIDE):
        mine = [stats[s, SEEN[s].index(k)] for s in range(SIDE)]
        top = functools.reduce(jnp.maximum, [m[0:1] for m in mine])
        weight = sum(m[1:2] * jnp.exp2((m[0:1] - top) * rate) for m in mine)
        scale = meta[k, 1:2, :] * inv_temp
        shift[0:1, block(k)] = top + (jnp.log2(weight) - jnp.log2(scale)) * (1.0 / rate)
        shift[1:2, block(k)] = scale
        if k == OWN:
            hit = sum(m[2:3] for m in mine)
            loss_ref[...] = ((top - hit) * inv_temp + jnp.log(weight)).reshape(rows)

    def coefficients(s, i0, cols):
        @pl.loop(0, rows // strip)
        def _(i):
            part = pl.ds(pl.multiple_of(s * rows + i * strip, strip), strip)
            for c in range(i0, i0 + cols, rows):
                lanes = pl.ds(c, rows)
                e = jnp.exp2((scores[part, lanes] - shift[0:1, lanes]) * rate)
                hit = lax.broadcasted_iota(jnp.int32, (strip, rows), 0) == pos_all[0:1, lanes] - (base(s) + i * strip)
                coef[part, lanes] = (e - jnp.where(hit, shift[1:2, lanes], 0.0)).astype(BF16)

    def turn(k):
        @pl.loop(0, SIDE)
        def _(s):
            part = pl.ds(pl.multiple_of(s * rows, rows), rows)
            coef_t[k * rows : (k + 1) * rows, part] = coef[part, k * rows : (k + 1) * rows].T

    def product(a, k):
        lhs = coef_t if a == 0 else coef
        return jnp.dot(lhs[k * rows : (k + 1) * rows, :], gathered[1 - a], preferred_element_type=F32)

    def rs(a, d, k):
        h = (d, d, 1 - d, d, d)[k]
        if k < 2:
            rows_of = pl.ds(h * half + k * quarter, quarter)
            src, dst = sent.at[a, 2, rows_of], hop1.at[a, d, pl.ds(k * quarter, quarter)]
        elif k == 2:
            rows_of = pl.ds(h * half, half)
            src, dst = sent.at[a, d, rows_of], hop2.at[a, d, rows_of]
        else:
            rows_of = pl.ds(h * half + (k - 3) * quarter, quarter)
            src, dst = sent.at[a, d, rows_of], hop2.at[a, d, rows_of]
        return remote(src, dst, rs_send.at[a, d, k], rs_recv.at[a, d, k], at(a, (PREV, NEXT)[d]))

    def far(a):
        sent[a, 2] = product(a, FAR).astype(BF16)
        for k in range(2):
            for d in range(2):
                rs(a, d, k).start()

    def near(a, d):
        r = product(a, (PREV, NEXT)[d])
        keep, send = (r[half:], r[:half]) if d == 1 else (r[:half], r[half:])
        partial[a, d] = keep
        sent[a, d, (1 - d) * half : (2 - d) * half, :] = send.astype(BF16)
        rs(a, d, 2).start()

    def own(a):
        (gq_ref, gp_ref)[a][...] = product(a, OWN)

    def pass_on(a, d, k):
        rs(a, d, k).wait_recv()
        rows_of = slice(d * half + k * quarter, d * half + (k + 1) * quarter)
        sent[a, d, rows_of, :] = (
            partial[a, d, k * quarter : (k + 1) * quarter, :]
            + hop1[a, d, k * quarter : (k + 1) * quarter, :].astype(F32)
        ).astype(BF16)
        rs(a, d, k + 3).start()

    coefficients(FAR, 0, total)
    far(1)
    for s in (OWN, NEXT, PREV):
        coefficients(s, 3 * rows, rows)
    turn(FAR)
    far(0)
    for s in (NEXT, PREV, OWN):
        coefficients(s, 0, 3 * rows)
    for d in range(2):
        near(1, d)
    turn(PREV)
    near(0, 0)
    turn(NEXT)
    near(0, 1)
    for k in range(2):
        for a in (1, 0):
            for d in range(2):
                pass_on(a, d, k)
    turn(OWN)
    own(1)
    own(0)

    def add(a, d, k):
        rs(a, d, k).wait_recv()
        out = (gq_ref, gp_ref)[a]
        h = (d, d, 1 - d, d, d)[k]
        start, size = (h * half, half) if k == 2 else (h * half + (k - 3) * quarter, quarter)
        out[start : start + size, :] += hop2[a, d, start : start + size, :].astype(F32)

    for k in (2, 3, 4):
        for a in (1, 0):
            for d in range(2):
                add(a, d, k)

    for a, d in pairs:
        ag(a, d, 3).wait_send()
        for k in range(5):
            rs(a, d, k).wait_send()


def deliver(*refs):
    n = len(refs) // 2
    copies = [pltpu.make_async_copy(refs[i], refs[n + i], refs[-1].at[i]) for i in range(n)]
    for copy in copies:
        copy.start()
    for copy in copies:
        copy.wait()


def per_device(queries, passages, positives, weights):
    rows, width = queries.shape
    total = SIDE * rows
    inv_temp = 2.0 / math.sqrt(width)
    vmem = pl.BlockSpec(memory_space=pltpu.VMEM)
    hbm = pl.BlockSpec(memory_space=pl.ANY)
    dma = pltpu.SemaphoreType.DMA
    results = pl.pallas_call(
        functools.partial(kernel, rows, width, inv_temp),
        out_shape=(
            pltpu.VMEM((rows,), F32),
            pltpu.VMEM((rows, width), F32),
            pltpu.VMEM((rows, width), F32),
        ),
        in_specs=[hbm, hbm, vmem, vmem],
        out_specs=(vmem, vmem, vmem),
        scratch_shapes=[
            pltpu.VMEM((2, rows, width), F32),
            pltpu.VMEM((2, total, width), BF16),
            pltpu.VMEM((total, total), F32),
            pltpu.VMEM((total, total), BF16),
            pltpu.VMEM((total, total), BF16),
            pltpu.VMEM((SIDE, 8, rows), F32),
            pltpu.VMEM((8, total), jnp.int32),
            pltpu.VMEM((SIDE, SIDE, 8, rows), F32),
            pltpu.VMEM((8, total), F32),
            pltpu.VMEM((8, total), F32),
            pltpu.VMEM((8, total), F32),
            pltpu.VMEM((8, total), F32),
            pltpu.VMEM((2, 2, rows // 2, width), F32),
            pltpu.VMEM((2, 3, rows, width), BF16),
            pltpu.VMEM((2, 2, rows // 2, width), BF16),
            pltpu.VMEM((2, 2, rows, width), BF16),
            dma((2,)),
            dma((2, 2, 4)),
            dma((2, 2, 4)),
            dma((SIDE,)),
            dma((SIDE,)),
            dma((SIDE,)),
            dma((SIDE,)),
            dma((2, 2, 5)),
            dma((2, 2, 5)),
            pltpu.SemaphoreType.REGULAR,
        ],
        compiler_params=pltpu.CompilerParams(
            collective_id=0, has_side_effects=True, vmem_limit_bytes=56 * 2**20
        ),
    )(queries, passages, positives, weights)
    return pl.pallas_call(
        deliver,
        out_shape=tuple(jax.ShapeDtypeStruct(r.shape, F32) for r in results),
        in_specs=[hbm] * 3,
        out_specs=(hbm,) * 3,
        scratch_shapes=[dma((3,))],
    )(*[pltpu.with_memory_space_constraint(r, pltpu.VMEM) for r in results])


def solution(mesh):
    split = P(("dp", "group"))
    whole = P(("dp", "group"), None)
    return jax.shard_map(
        per_device,
        mesh=mesh,
        in_specs=(whole, whole, split, split),
        out_specs=(split, whole, whole),
        check_vma=False,
    )
```

```python
import functools
import math

import jax
import jax.numpy as jnp
from jax import lax
from jax.experimental import pallas as pl
from jax.experimental.pallas import tpu as pltpu
from jax.sharding import PartitionSpec as P

MESH = pl.DeviceIdType.MESH
SIDE = 4
OWN, NEXT, PREV, FAR = range(4)
STEP = (0, 1, 3, 2)
SEEN = tuple(tuple(STEP.index((STEP[s] + STEP[k]) % SIDE) for k in range(SIDE)) for s in range(SIDE))
LOG2E = math.log2(math.e)
BF16, F32 = jnp.bfloat16, jnp.float32


def kernel(
    rows, width, inv_temp,
    q_hbm, p_hbm, pos_ref, w_ref,
    loss_ref, gq_ref, gp_ref,
    stage, gathered, scores, coef, meta, pos_all, stats, peak, mass, found, shift, sent, hop1, hop2,
    load_sem, ag_send, ag_recv, meta_send, meta_recv, st_send, st_recv, rs_send, rs_recv, go_sem,
):
    half, quarter = rows // 2, rows // 4
    total = SIDE * rows
    rate = inv_temp * LOG2E
    dp, me = lax.axis_index("dp"), lax.axis_index("group")
    z, y = me // SIDE, me % SIDE
    first = dp % 2 == 0
    sibling = dp + 1 - 2 * (dp % 2)

    def at(axis, slot):
        if axis == 0:
            return (dp, z * SIDE + (y + STEP[slot]) % SIDE)
        return (dp, (z + STEP[slot]) % SIDE * SIDE + y)

    greet = [at(0, NEXT), at(0, PREV), at(0, FAR), at(1, NEXT), at(1, PREV), (sibling, me)]
    barrier = pltpu.get_barrier_semaphore()
    for device in greet:
        pl.semaphore_signal(barrier, inc=1, device_id=device, device_id_type=MESH)

    def load(a, n):
        part = pl.ds(n * quarter, quarter)
        return pltpu.make_async_copy((q_hbm, p_hbm)[a].at[part], stage.at[a, part], load_sem.at[a, n])

    order = [(a, d, k) for k in range(2) for d in range(2) for a in (1, 0)]
    for a, d, k in order:
        load(a, 2 * d + k).start()
    meta[OWN] = jnp.zeros(meta.shape[1:], F32)
    meta[OWN, 0:1, :] = pos_ref[...].reshape(1, rows).astype(F32)
    meta[OWN, 1:2, :] = w_ref[...].reshape(1, rows)

    def block(slot):
        return pl.ds(slot * rows, rows)

    def remote(src, dst, send, recv, device):
        return pltpu.make_async_remote_copy(
            src_ref=src, dst_ref=dst, send_sem=send, recv_sem=recv, device_id=device, device_id_type=MESH
        )

    metas = [
        remote(meta.at[OWN], meta.at[STEP.index(-STEP[s] % SIDE)], meta_send.at[s], meta_recv.at[s], at(0, s))
        for s in (NEXT, PREV, FAR)
    ]
    def ag(a, d, k):
        near = (NEXT, PREV)[d]
        start, size = ((1 - d) * half, half) if k == 2 else (d * half + k % 3 * quarter, quarter)
        src, dst = (OWN, near) if k < 3 else (near, FAR)
        src, dst = (pl.ds(slot * rows + start, size) for slot in (src, dst))
        return remote(
            gathered.at[a, src], gathered.at[a, dst],
            ag_send.at[a, d, k], ag_recv.at[a, d, k], at(a, (PREV, NEXT)[d]),
        )

    pairs = [(a, d) for d in range(2) for a in (1, 0)]

    def cast(a, n):
        load(a, n).wait()

        @pl.loop(0, quarter // 16)
        def _(i):
            part = pl.ds(pl.multiple_of(n * quarter + i * 16, 16), 16)
            gathered[a, part, :] = stage[a, part, :].astype(BF16)

    @pl.when(first)
    def _():
        for n, (a, d, k) in enumerate(order):
            cast(a, 2 * d + k)
            if n == 0:
                pl.semaphore_wait(barrier, len(greet))
            ag(a, d, k).start()
        for a, d in pairs:
            ag(a, d, 2).start()
        for copy in metas:
            copy.start()

    @pl.when(jnp.logical_not(first))
    def _():
        for a, d, k in order:
            cast(a, 2 * d + k)
        pl.semaphore_wait(barrier, len(greet))
        for copy in metas:
            copy.start()
        pl.semaphore_wait(go_sem, 1)
        for k in range(3):
            for a, d in pairs:
                ag(a, d, k).start()

    def base(slot):
        owner = (z + STEP[slot]) % SIDE * SIDE + y
        return owner * rows

    def score(j0, i0, deep, wide):
        r = lax.dot_general(
            gathered[1, j0 : j0 + deep, :], gathered[0, i0 : i0 + wide, :], (((1,), (1,)), ((), ())),
            preferred_element_type=F32,
        )
        scores[j0 : j0 + deep, i0 : i0 + wide] = r
        top = jnp.max(r.reshape(deep // 8, 8, wide), axis=0)
        peak[:, i0 : i0 + wide] = jnp.maximum(peak[:, i0 : i0 + wide], top)

    def settle(i0, wide):
        cols = slice(i0, i0 + wide)
        top = jnp.max(peak[:, cols], axis=0, keepdims=True)
        mass[:, cols] = mass[:, cols] * jnp.exp2((shift[0:1, cols] - top) * rate)
        shift[0:1, cols] = top

    strip = 64 if rows % 64 == 0 else rows

    def accumulate(s, i0, cols):
        @pl.loop(0, rows // strip)
        def _(i):
            part = pl.ds(pl.multiple_of(s * rows + i * strip, strip), strip)
            for c in range(i0, i0 + cols, rows):
                lanes = pl.ds(c, rows)
                r = scores[part, lanes]
                e = jnp.exp2((r - shift[0:1, lanes]) * rate)
                scores[part, lanes] = e
                hit = lax.broadcasted_iota(jnp.int32, (strip, rows), 0) == pos_all[0:1, lanes] - (base(s) + i * strip)
                g = jnp.where(hit, r, 0.0)
                mass[:, lanes] += jnp.sum(e.reshape(strip // 8, 8, rows), axis=0)
                found[:, lanes] += jnp.sum(g.reshape(strip // 8, 8, rows), axis=0)

    peak[...] = jnp.full(peak.shape, -jnp.inf, F32)
    shift[...] = jnp.full(shift.shape, -jnp.inf, F32)
    mass[...] = jnp.zeros(mass.shape, F32)
    found[...] = jnp.zeros(found.shape, F32)
    score(0, 0, rows, rows)

    for k in range(2):
        for a, d in pairs:
            ag(a, d, k).wait_recv()
            ag(a, d, k + 3).start()
    for a, d in pairs:
        for k in range(4):
            ag(a, d, k).wait_send()

    @pl.when(first)
    def _():
        pl.semaphore_signal(go_sem, inc=1, device_id=(sibling, me), device_id_type=MESH)

    for copy in metas:
        copy.wait()
    for s in range(SIDE):
        pos_all[:, block(s)] = jnp.broadcast_to(meta[s, 0:1, :], (8, rows)).astype(jnp.int32)
    for a, d in pairs:
        ag(a, d, 2).wait_recv()

    score(rows, 0, 2 * rows, 3 * rows)
    score(0, rows, rows, 2 * rows)
    settle(0, 3 * rows)
    for s in (OWN, NEXT, PREV):
        accumulate(s, 0, 3 * rows)

    for a, d in pairs:
        for k in (3, 4):
            ag(a, d, k).wait_recv()

    score(3 * rows, 0, rows, 2 * rows)
    score(3 * rows, 2 * rows, rows, 2 * rows)
    score(0, 3 * rows, 3 * rows, rows)
    shift[1:2, :] = shift[0:1, :]
    settle(0, total)
    accumulate(FAR, 0, total)
    for s in (OWN, NEXT, PREV):
        accumulate(s, 3 * rows, rows)

    for s in range(SIDE):
        cols = block(s)
        stats[OWN, 0, s : s + 1, :] = shift[0:1, cols]
        stats[OWN, 0, SIDE + s : SIDE + s + 1, :] = jnp.sum(mass[:, cols], axis=0, keepdims=True)
        stats[OWN, 1, s : s + 1, :] = jnp.sum(found[:, cols], axis=0, keepdims=True)
    posts, late_posts = (
        [
            remote(stats.at[OWN, n], stats.at[STEP.index(-STEP[s] % SIDE), n], st_send.at[n, s], st_recv.at[n, s], at(0, s))
            for s in (NEXT, PREV, FAR)
        ]
        for n in range(2)
    )
    for copy in posts + late_posts:
        copy.start()

    def product(a, k, start, size, part=None):
        rhs = gathered[1 - a, :, start : start + size]
        if a == 0:
            lhs = coef[:, k * rows : (k + 1) * rows]
            return lax.dot_general(lhs, rhs, (((0,), (0,)), ((), ())), preferred_element_type=F32)
        first_row, end = part or (0, rows)
        return jnp.dot(coef[k * rows + first_row : k * rows + end, :], rhs, preferred_element_type=F32)

    for s in range(SIDE):

        @pl.loop(0, rows // strip)
        def _(i):
            part = pl.ds(pl.multiple_of(s * rows + i * strip, strip), strip)
            coef[part, block(FAR)] = scores[part, block(FAR)].astype(BF16)
            hit = lax.broadcasted_iota(jnp.int32, (strip, rows), 0) == pos_all[0:1, block(FAR)] - (base(s) + i * strip)
            coef[part, block(OWN)] = jnp.where(hit, 1.0, 0.0).astype(BF16)

    stage[0] = product(0, FAR, 0, width)
    stage[1] = product(0, OWN, 0, width)

    for copy in posts:
        copy.wait()
    for k in range(SIDE):
        mine = [stats[s, 0] for s in range(SIDE)]
        places = [SEEN[s].index(k) for s in range(SIDE)]
        tops = [m[p : p + 1] for m, p in zip(mine, places)]
        top = functools.reduce(jnp.maximum, tops)
        weight = sum(
            m[SIDE + p : SIDE + p + 1] * jnp.exp2((t - top) * rate) for m, p, t in zip(mine, places, tops)
        )
        scale = meta[k, 1:2, :] * inv_temp
        for n in range(2):
            shift[2 + n : 3 + n, block(k)] = jnp.exp2((shift[n : n + 1, block(k)] - top) * rate) * (scale / weight)
        shift[4:5, block(k)] = scale
        if k == OWN:
            peak[0:1, block(OWN)] = top * inv_temp + jnp.log(weight)

    def coefficients(s, i0, cols):
        n = 0 if s == FAR or i0 == 3 * rows else 1

        @pl.loop(0, rows // strip)
        def _(i):
            part = pl.ds(pl.multiple_of(s * rows + i * strip, strip), strip)
            for c in range(i0, i0 + cols, rows):
                lanes = pl.ds(c, rows)
                e = scores[part, lanes] * shift[2 + n : 3 + n, lanes]
                hit = lax.broadcasted_iota(jnp.int32, (strip, rows), 0) == pos_all[0:1, lanes] - (base(s) + i * strip)
                coef[part, lanes] = (e - jnp.where(hit, shift[4:5, lanes], 0.0)).astype(BF16)

    side = width // 2

    def rs(a, d, k):
        rows_of = pl.ds((k if k < 2 else k - 3) * half, half)
        if k < 2:
            src, dst = sent.at[a, 2, d, rows_of], hop1.at[a, d, rows_of]
        elif k == 2:
            src, dst = sent.at[a, d, 1 - d], hop2.at[a, d, 1 - d]
        else:
            src, dst = sent.at[a, d, d, rows_of], hop2.at[a, d, d, rows_of]
        return remote(src, dst, rs_send.at[a, d, k], rs_recv.at[a, d, k], at(a, (PREV, NEXT)[d]))

    def far_passages(d, k):
        part = slice(k * half, (k + 1) * half)
        sent[1, 2, d, part, :] = product(1, FAR, d * side, side, (k * half, (k + 1) * half)).astype(BF16)
        rs(1, d, k).start()

    def far_queries():
        factors = shift[:, block(FAR)].T
        for d in range(2):
            cols = slice(d * side, (d + 1) * side)
            sent[0, 2, d] = (stage[0, :, cols] * factors[:, 2:3] - stage[1, :, cols] * factors[:, 4:5]).astype(BF16)
            for k in range(2):
                rs(0, d, k).start()

    def near(a, d):
        sent[a, d, 1 - d] = product(a, (PREV, NEXT)[d], (1 - d) * side, side).astype(BF16)
        rs(a, d, 2).start()

    def pass_on(a, d):
        r = product(a, (PREV, NEXT)[d], d * side, side)
        for k in range(2):
            rs(a, d, k).wait_recv()
            part = slice(k * half, (k + 1) * half)
            sent[a, d, d, part, :] = (r[part] + hop1[a, d, part, :].astype(F32)).astype(BF16)
            rs(a, d, k + 3).start()

    coefficients(FAR, 0, total)
    for d in range(2):
        far_passages(d, 0)
    far_queries()
    for d in range(2):
        far_passages(d, 1)
    for s in (NEXT, PREV, OWN):
        coefficients(s, 3 * rows, rows)
        coefficients(s, 0, 3 * rows)
    for a in (1, 0):
        for d in range(2):
            near(a, d)
    for a in (1, 0):
        for d in range(2):
            pass_on(a, d)
    for a in (1, 0):
        (gq_ref, gp_ref)[a][...] = product(a, OWN, 0, width)
    for copy in late_posts:
        copy.wait()
    hit = sum(stats[s, 1, SEEN[s].index(OWN) : SEEN[s].index(OWN) + 1, :] for s in range(SIDE))
    loss_ref[...] = (peak[0:1, block(OWN)] - hit * inv_temp).reshape(rows)

    def add(a, d, k):
        rs(a, d, k).wait_recv()
        out = (gq_ref, gp_ref)[a]
        h = 1 - d if k == 2 else d
        part = slice(0, rows) if k == 2 else slice((k - 3) * half, (k - 2) * half)
        out[part, h * side : (h + 1) * side] += hop2[a, d, h, part, :].astype(F32)

    for k in (2, 3, 4):
        for a in (1, 0):
            for d in range(2):
                add(a, d, k)

    for a, d in pairs:
        ag(a, d, 4).wait_send()
        for k in range(5):
            rs(a, d, k).wait_send()


def deliver(*refs):
    n = len(refs) // 2
    copies = [pltpu.make_async_copy(refs[i], refs[n + i], refs[-1].at[i]) for i in range(n)]
    for copy in copies:
        copy.start()
    for copy in copies:
        copy.wait()


def per_device(queries, passages, positives, weights):
    rows, width = queries.shape
    total = SIDE * rows
    inv_temp = 2.0 / math.sqrt(width)
    vmem = pl.BlockSpec(memory_space=pltpu.VMEM)
    hbm = pl.BlockSpec(memory_space=pl.ANY)
    dma = pltpu.SemaphoreType.DMA
    results = pl.pallas_call(
        functools.partial(kernel, rows, width, inv_temp),
        out_shape=(
            pltpu.VMEM((rows,), F32),
            pltpu.VMEM((rows, width), F32),
            pltpu.VMEM((rows, width), F32),
        ),
        in_specs=[hbm, hbm, vmem, vmem],
        out_specs=(vmem, vmem, vmem),
        scratch_shapes=[
            pltpu.VMEM((2, rows, width), F32),
            pltpu.VMEM((2, total, width), BF16),
            pltpu.VMEM((total, total), F32),
            pltpu.VMEM((total, total), BF16),
            pltpu.VMEM((SIDE, 8, rows), F32),
            pltpu.VMEM((8, total), jnp.int32),
            pltpu.VMEM((SIDE, 2, 2 * SIDE, rows), F32),
            pltpu.VMEM((8, total), F32),
            pltpu.VMEM((8, total), F32),
            pltpu.VMEM((8, total), F32),
            pltpu.VMEM((8, total), F32),
            pltpu.VMEM((2, 3, 2, rows, width // 2), BF16),
            pltpu.VMEM((2, 2, rows, width // 2), BF16),
            pltpu.VMEM((2, 2, 2, rows, width // 2), BF16),
            dma((2, 4)),
            dma((2, 2, 5)),
            dma((2, 2, 5)),
            dma((SIDE,)),
            dma((SIDE,)),
            dma((2, SIDE)),
            dma((2, SIDE)),
            dma((2, 2, 5)),
            dma((2, 2, 5)),
            pltpu.SemaphoreType.REGULAR,
        ],
        compiler_params=pltpu.CompilerParams(
            collective_id=0, has_side_effects=True, vmem_limit_bytes=56 * 2**20
        ),
    )(queries, passages, positives, weights)
    return pl.pallas_call(
        deliver,
        out_shape=tuple(jax.ShapeDtypeStruct(r.shape, F32) for r in results),
        in_specs=[hbm] * 3,
        out_specs=(hbm,) * 3,
        scratch_shapes=[dma((3,))],
    )(*[pltpu.with_memory_space_constraint(r, pltpu.VMEM) for r in results])


def solution(mesh):
    split = P(("dp", "group"))
    whole = P(("dp", "group"), None)
    return jax.shard_map(
        per_device,
        mesh=mesh,
        in_specs=(whole, whole, split, split),
        out_specs=(split, whole, whole),
        check_vma=False,
    )
```

```python
import functools
import math

import jax
import jax.numpy as jnp
from jax import lax
from jax.experimental import pallas as pl
from jax.experimental.pallas import tpu as pltpu
from jax.sharding import PartitionSpec as P

MESH = pl.DeviceIdType.MESH
SIDE = 4
OWN, NEXT, PREV, FAR = range(4)
STEP = (0, 1, 3, 2)
SEEN = tuple(tuple(STEP.index((STEP[s] + STEP[k]) % SIDE) for k in range(SIDE)) for s in range(SIDE))
LOG2E = math.log2(math.e)
BF16, F32 = jnp.bfloat16, jnp.float32


def kernel(
    rows, width, inv_temp,
    q_hbm, p_hbm, pos_ref, w_ref,
    loss_ref, gq_ref, gp_ref,
    stage, gathered, scores, terms, coef, meta, pos_all, stats, peak, mass, found, shift, sent, hop1, hop2,
    load_sem, ag_send, ag_recv, meta_send, meta_recv, st_send, st_recv, rs_send, rs_recv, go_sem,
):
    half, quarter = rows // 2, rows // 4
    total = SIDE * rows
    rate = inv_temp * LOG2E
    dp, me = lax.axis_index("dp"), lax.axis_index("group")
    z, y = me // SIDE, me % SIDE
    first = dp % 2 == 0
    sibling = dp + 1 - 2 * (dp % 2)

    def at(axis, slot):
        if axis == 0:
            return (dp, z * SIDE + (y + STEP[slot]) % SIDE)
        return (dp, (z + STEP[slot]) % SIDE * SIDE + y)

    greet = [at(0, NEXT), at(0, PREV), at(0, FAR), at(1, NEXT), at(1, PREV), (sibling, me)]
    barrier = pltpu.get_barrier_semaphore()
    for device in greet:
        pl.semaphore_signal(barrier, inc=1, device_id=device, device_id_type=MESH)

    def load(a, n):
        part = pl.ds(n * quarter, quarter)
        return pltpu.make_async_copy((q_hbm, p_hbm)[a].at[part], stage.at[a, part], load_sem.at[a, n])

    order = [(a, d, k) for k in range(2) for d in range(2) for a in (1, 0)]
    for a, d, k in order:
        load(a, 2 * d + k).start()
    meta[OWN] = jnp.zeros(meta.shape[1:], F32)
    meta[OWN, 0:1, :] = pos_ref[...].reshape(1, rows).astype(F32)
    meta[OWN, 1:2, :] = w_ref[...].reshape(1, rows)

    def block(slot):
        return pl.ds(slot * rows, rows)

    def remote(src, dst, send, recv, device):
        return pltpu.make_async_remote_copy(
            src_ref=src, dst_ref=dst, send_sem=send, recv_sem=recv, device_id=device, device_id_type=MESH
        )

    metas = [
        remote(meta.at[OWN], meta.at[STEP.index(-STEP[s] % SIDE)], meta_send.at[s], meta_recv.at[s], at(0, s))
        for s in (NEXT, PREV, FAR)
    ]
    def ag(a, d, k):
        near = (NEXT, PREV)[d]
        start, size = ((1 - d) * half, half) if k == 2 else (d * half + k % 3 * quarter, quarter)
        src, dst = (OWN, near) if k < 3 else (near, FAR)
        src, dst = (pl.ds(slot * rows + start, size) for slot in (src, dst))
        return remote(
            gathered.at[a, src], gathered.at[a, dst],
            ag_send.at[a, d, k], ag_recv.at[a, d, k], at(a, (PREV, NEXT)[d]),
        )

    pairs = [(a, d) for d in range(2) for a in (1, 0)]

    def cast(a, n):
        load(a, n).wait()

        @pl.loop(0, quarter // 16)
        def _(i):
            part = pl.ds(pl.multiple_of(n * quarter + i * 16, 16), 16)
            gathered[a, part, :] = stage[a, part, :].astype(BF16)

    @pl.when(first)
    def _():
        for n, (a, d, k) in enumerate(order):
            cast(a, 2 * d + k)
            if n == 0:
                pl.semaphore_wait(barrier, len(greet))
                for copy in metas:
                    copy.start()
            ag(a, d, k).start()
        for a, d in pairs:
            ag(a, d, 2).start()

    @pl.when(jnp.logical_not(first))
    def _():
        for a, d, k in order:
            cast(a, 2 * d + k)
        pl.semaphore_wait(barrier, len(greet))
        for copy in metas:
            copy.start()
        pl.semaphore_wait(go_sem, 1)
        for k in range(3):
            for a, d in pairs:
                ag(a, d, k).start()

    def base(slot):
        owner = (z + STEP[slot]) % SIDE * SIDE + y
        return owner * rows

    def score(j0, i0, deep, wide):
        r = lax.dot_general(
            gathered[1, j0 : j0 + deep, :], gathered[0, i0 : i0 + wide, :], (((1,), (1,)), ((), ())),
            preferred_element_type=F32,
        )
        scores[j0 : j0 + deep, i0 : i0 + wide] = r
        top = jnp.max(r.reshape(deep // 8, 8, wide), axis=0)
        peak[:, i0 : i0 + wide] = jnp.maximum(peak[:, i0 : i0 + wide], top)

    def settle(i0, wide):
        cols = slice(i0, i0 + wide)
        top = jnp.max(peak[:, cols], axis=0, keepdims=True)
        mass[:, cols] = mass[:, cols] * jnp.exp2((shift[0:1, cols] - top) * rate)
        shift[0:1, cols] = top

    strip = 64 if rows % 64 == 0 else rows

    def accumulate(s, i0, cols):
        @pl.loop(0, rows // strip)
        def _(i):
            part = pl.ds(pl.multiple_of(s * rows + i * strip, strip), strip)
            for c in range(i0, i0 + cols, rows):
                lanes = pl.ds(c, rows)
                r = scores[part, lanes]
                e = jnp.exp2((r - shift[0:1, lanes]) * rate)
                terms[part, lanes] = e
                if c == 3 * rows:
                    coef[part, lanes] = e.astype(BF16)
                mass[:, lanes] += jnp.sum(e.reshape(strip // 8, 8, rows), axis=0)

    def seek():
        for s in range(SIDE):

            @pl.loop(0, rows // strip)
            def _(i):
                part = pl.ds(pl.multiple_of(s * rows + i * strip, strip), strip)
                for c in range(0, total, rows):
                    lanes = pl.ds(c, rows)
                    hit = lax.broadcasted_iota(jnp.int32, (strip, rows), 0) == pos_all[0:1, lanes] - (base(s) + i * strip)
                    g = jnp.where(hit, scores[part, lanes], 0.0)
                    found[:, lanes] += jnp.sum(g.reshape(strip // 8, 8, rows), axis=0)

        for s in range(SIDE):
            stats[OWN, 1, s : s + 1, :] = jnp.sum(found[:, block(s)], axis=0, keepdims=True)
        for copy in late_posts:
            copy.start()

    def product(a, k, start, size, part=None):
        rhs = gathered[1 - a, :, start : start + size]
        if a == 0:
            lhs = coef[:, k * rows : (k + 1) * rows]
            return lax.dot_general(lhs, rhs, (((0,), (0,)), ((), ())), preferred_element_type=F32)
        first_row, end = part or (0, rows)
        return jnp.dot(coef[k * rows + first_row : k * rows + end, :], rhs, preferred_element_type=F32)

    peak[...] = jnp.full(peak.shape, -jnp.inf, F32)
    shift[...] = jnp.full(shift.shape, -jnp.inf, F32)
    mass[...] = jnp.zeros(mass.shape, F32)
    found[...] = jnp.zeros(found.shape, F32)
    score(0, 0, rows, rows)

    for k in range(2):
        for a, d in pairs:
            ag(a, d, k).wait_recv()
            ag(a, d, k + 3).start()
    for a, d in pairs:
        for k in range(4):
            ag(a, d, k).wait_send()

    @pl.when(first)
    def _():
        pl.semaphore_signal(go_sem, inc=1, device_id=(sibling, me), device_id_type=MESH)

    for copy in metas:
        copy.wait()
    for s in range(SIDE):
        pos_all[:, block(s)] = jnp.broadcast_to(meta[s, 0:1, :], (8, rows)).astype(jnp.int32)

    for s in range(SIDE):

        @pl.loop(0, rows // strip)
        def _(i):
            part = pl.ds(pl.multiple_of(s * rows + i * strip, strip), strip)
            hit = lax.broadcasted_iota(jnp.int32, (strip, rows), 0) == pos_all[0:1, block(FAR)] - (base(s) + i * strip)
            coef[part, block(OWN)] = jnp.where(hit, 1.0, 0.0).astype(BF16)

    def hits(start, end):
        return lax.dot_general(
            coef[start:end, block(OWN)], gathered[1, start:end, :], (((0,), (0,)), ((), ())), preferred_element_type=F32
        )

    early = rows + (rows // 3 if rows % 3 == 0 else rows // 2)
    stage[1] = hits(0, early)
    for a, d in pairs:
        ag(a, d, 2).wait_recv()

    score(rows, 0, 2 * rows, 3 * rows)
    score(0, rows, rows, 2 * rows)
    settle(0, 3 * rows)
    for s in (OWN, NEXT, PREV):
        accumulate(s, 0, 3 * rows)

    for a, d in pairs:
        for k in (3, 4):
            ag(a, d, k).wait_recv()

    score(3 * rows, 0, rows, 2 * rows)
    score(3 * rows, 2 * rows, rows, 2 * rows)
    score(0, 3 * rows, 3 * rows, rows)
    shift[1:2, :] = shift[0:1, :]
    settle(0, total)
    accumulate(FAR, 0, total)
    for s in (OWN, NEXT, PREV):
        accumulate(s, 3 * rows, rows)

    for s in range(SIDE):
        cols = block(s)
        stats[OWN, 0, s : s + 1, :] = shift[0:1, cols]
        stats[OWN, 0, SIDE + s : SIDE + s + 1, :] = jnp.sum(mass[:, cols], axis=0, keepdims=True)
    posts, late_posts = (
        [
            remote(stats.at[OWN, n], stats.at[STEP.index(-STEP[s] % SIDE), n], st_send.at[n, s], st_recv.at[n, s], at(0, s))
            for s in (NEXT, PREV, FAR)
        ]
        for n in range(2)
    )
    for copy in posts:
        copy.start()

    stage[0] = product(0, FAR, 0, width)
    stage[1] = stage[1] + hits(early, total)
    seek()

    for copy in posts:
        copy.wait()
    for k in range(SIDE):
        mine = [stats[s, 0] for s in range(SIDE)]
        places = [SEEN[s].index(k) for s in range(SIDE)]
        tops = [m[p : p + 1] for m, p in zip(mine, places)]
        top = functools.reduce(jnp.maximum, tops)
        weight = sum(
            m[SIDE + p : SIDE + p + 1] * jnp.exp2((t - top) * rate) for m, p, t in zip(mine, places, tops)
        )
        scale = meta[k, 1:2, :] * inv_temp
        for n in range(2):
            shift[2 + n : 3 + n, block(k)] = jnp.exp2((shift[n : n + 1, block(k)] - top) * rate) * (scale / weight)
        shift[4:5, block(k)] = scale
        if k == OWN:
            peak[0:1, block(OWN)] = top * inv_temp + jnp.log(weight)

    def coefficients(s, i0, cols):
        n = 0 if s == FAR or i0 == 3 * rows else 1

        @pl.loop(0, rows // strip)
        def _(i):
            part = pl.ds(pl.multiple_of(s * rows + i * strip, strip), strip)
            for c in range(i0, i0 + cols, rows):
                lanes = pl.ds(c, rows)
                e = terms[part, lanes] * shift[2 + n : 3 + n, lanes]
                hit = lax.broadcasted_iota(jnp.int32, (strip, rows), 0) == pos_all[0:1, lanes] - (base(s) + i * strip)
                coef[part, lanes] = (e - jnp.where(hit, shift[4:5, lanes], 0.0)).astype(BF16)

    side = width // 2

    def rs(a, d, k):
        rows_of = pl.ds((k if k < 2 else k - 3) * half, half)
        if k < 2:
            src, dst = sent.at[a, 2, d, rows_of], hop1.at[a, d, rows_of]
        elif k == 2:
            src, dst = sent.at[a, d, 1 - d], hop2.at[a, d, 1 - d]
        else:
            src, dst = sent.at[a, d, d, rows_of], hop2.at[a, d, d, rows_of]
        return remote(src, dst, rs_send.at[a, d, k], rs_recv.at[a, d, k], at(a, (PREV, NEXT)[d]))

    def far_passages(k):
        part = slice(k * half, (k + 1) * half)
        r = product(1, FAR, 0, width, (k * half, (k + 1) * half)).astype(BF16)
        for d in range(2):
            sent[1, 2, d, part, :] = r[:, d * side : (d + 1) * side]
        for d in range(2):
            rs(1, d, k).start()

    def far_queries():
        factors = shift[:, block(FAR)].T
        for d in range(2):
            cols = slice(d * side, (d + 1) * side)
            sent[0, 2, d] = (stage[0, :, cols] * factors[:, 2:3] - stage[1, :, cols] * factors[:, 4:5]).astype(BF16)
            for k in range(2):
                rs(0, d, k).start()

    def near(a, d):
        sent[a, d, 1 - d] = product(a, (PREV, NEXT)[d], (1 - d) * side, side).astype(BF16)
        rs(a, d, 2).start()

    def pass_on(a, d):
        r = product(a, (PREV, NEXT)[d], d * side, side)
        for k in range(2):
            rs(a, d, k).wait_recv()
            part = slice(k * half, (k + 1) * half)
            sent[a, d, d, part, :] = (r[part] + hop1[a, d, part, :].astype(F32)).astype(BF16)
            rs(a, d, k + 3).start()

    coefficients(FAR, 0, total)
    far_passages(0)
    far_queries()
    far_passages(1)
    for s in (NEXT, PREV, OWN):
        coefficients(s, 3 * rows, rows)
        coefficients(s, 0, 3 * rows)
    for a in (1, 0):
        for d in range(2):
            near(a, d)
    for a in (1, 0):
        for d in range(2):
            pass_on(a, d)
    for a in (1, 0):
        (gq_ref, gp_ref)[a][...] = product(a, OWN, 0, width)
    for copy in late_posts:
        copy.wait()
    hit = sum(stats[s, 1, SEEN[s].index(OWN) : SEEN[s].index(OWN) + 1, :] for s in range(SIDE))
    loss_ref[...] = (peak[0:1, block(OWN)] - hit * inv_temp).reshape(rows)

    def add(a, d, k):
        rs(a, d, k).wait_recv()
        out = (gq_ref, gp_ref)[a]
        h = 1 - d if k == 2 else d
        part = slice(0, rows) if k == 2 else slice((k - 3) * half, (k - 2) * half)
        out[part, h * side : (h + 1) * side] += hop2[a, d, h, part, :].astype(F32)

    for k in (2, 3, 4):
        for a in (1, 0):
            for d in range(2):
                add(a, d, k)

    for a, d in pairs:
        ag(a, d, 4).wait_send()
        for k in range(5):
            rs(a, d, k).wait_send()


def deliver(*refs):
    n = len(refs) // 2
    copies = [pltpu.make_async_copy(refs[i], refs[n + i], refs[-1].at[i]) for i in range(n)]
    for copy in copies:
        copy.start()
    for copy in copies:
        copy.wait()


def per_device(queries, passages, positives, weights):
    rows, width = queries.shape
    total = SIDE * rows
    inv_temp = 2.0 / math.sqrt(width)
    vmem = pl.BlockSpec(memory_space=pltpu.VMEM)
    hbm = pl.BlockSpec(memory_space=pl.ANY)
    dma = pltpu.SemaphoreType.DMA
    results = pl.pallas_call(
        functools.partial(kernel, rows, width, inv_temp),
        out_shape=(
            pltpu.VMEM((rows,), F32),
            pltpu.VMEM((rows, width), F32),
            pltpu.VMEM((rows, width), F32),
        ),
        in_specs=[hbm, hbm, vmem, vmem],
        out_specs=(vmem, vmem, vmem),
        scratch_shapes=[
            pltpu.VMEM((2, rows, width), F32),
            pltpu.VMEM((2, total, width), BF16),
            pltpu.VMEM((total, total), F32),
            pltpu.VMEM((total, total), F32),
            pltpu.VMEM((total, total), BF16),
            pltpu.VMEM((SIDE, 8, rows), F32),
            pltpu.VMEM((8, total), jnp.int32),
            pltpu.VMEM((SIDE, 2, 2 * SIDE, rows), F32),
            pltpu.VMEM((8, total), F32),
            pltpu.VMEM((8, total), F32),
            pltpu.VMEM((8, total), F32),
            pltpu.VMEM((8, total), F32),
            pltpu.VMEM((2, 3, 2, rows, width // 2), BF16),
            pltpu.VMEM((2, 2, rows, width // 2), BF16),
            pltpu.VMEM((2, 2, 2, rows, width // 2), BF16),
            dma((2, 4)),
            dma((2, 2, 5)),
            dma((2, 2, 5)),
            dma((SIDE,)),
            dma((SIDE,)),
            dma((2, SIDE)),
            dma((2, SIDE)),
            dma((2, 2, 5)),
            dma((2, 2, 5)),
            pltpu.SemaphoreType.REGULAR,
        ],
        compiler_params=pltpu.CompilerParams(
            collective_id=0, has_side_effects=True, vmem_limit_bytes=56 * 2**20
        ),
    )(queries, passages, positives, weights)
    return pl.pallas_call(
        deliver,
        out_shape=tuple(jax.ShapeDtypeStruct(r.shape, F32) for r in results),
        in_specs=[hbm] * 3,
        out_specs=(hbm,) * 3,
        scratch_shapes=[dma((3,))],
    )(*[pltpu.with_memory_space_constraint(r, pltpu.VMEM) for r in results])


def solution(mesh):
    split = P(("dp", "group"))
    whole = P(("dp", "group"), None)
    return jax.shard_map(
        per_device,
        mesh=mesh,
        in_specs=(whole, whole, split, split),
        out_specs=(split, whole, whole),
        check_vma=False,
    )
```
